128 devices in a mesh: ctx: 32 (over z, y, core), tp: 4 (over x).
Axes of the slice: x: 4, y: 4, z: 4, core: 2. Of those that a mesh axis runs over, the one named last changes fastest.
Arguments:
- queries: bfloat16 [16384, 8192], P('ctx', 'tp'), may hold values from -6 to 6
- keys: bfloat16 [16384, 1024], P('ctx', 'tp'), may hold values from -6 to 6
- values: bfloat16 [16384, 1024], P('ctx', 'tp'), may hold values from -6 to 6
- block_plan: int32 [32, 4], replicated, may hold values from 0 to 7, as said below
- doc_lengths: int32 [64], replicated, may hold values from 1 to 4096, 16384 in all
- scan_input: bfloat16 [16384, 16384], P('ctx', 'tp'), may hold values from -6 to 6
- gate_input: bfloat16 [16384, 16384], P('ctx', 'tp'), may hold values from -600 to 600
- step_size: bfloat16 [16384, 256], P('ctx', 'tp'), may hold values from 0 to 6
- decay_rate: float32 [256], P('tp'), may hold values from 0.05 to 1.5
- state_in: bfloat16 [16384, 16], P('ctx'), may hold values from -6 to 6
- state_out: bfloat16 [16384, 16], P('ctx'), may hold values from -6 to 6
- skip_gain: float32 [256], P('tp'), may hold values from 0.5 to 1.5
- norm_gain: float32 [16384], P('tp'), may hold values from 0.5 to 1.5
Outputs:
- attn_out: bfloat16 [16384, 8192], P('ctx', 'tp')
- mamba_out: bfloat16 [16384, 16384], P('ctx', 'tp')
The draws below stay inside these ranges and needn't reach their ends.
Inputs may be any that keep to these rules, and one draw needn't show every extreme that they name: `block_plan`: each row lists 4 distinct offsets, the first of them 0.
All inputs are finite; a program needn't handle non-finite values.
Results may differ from the reference program's by a relative error of at most 0.007.
Values may be sent and summed in bfloat16 or wider, within the bound.
No kernel may reach another device: no remote copies, remote signals or barrier semaphores. Data moves between devices by JAX's collectives and lax.ppermute only.
A program may use at most 128 MiB of HBM per device.

```python
import math
import jax
import jax.numpy as jnp
import numpy as np
from jax import lax

QUERY_HEADS = 64
KEY_VALUE_HEADS = 8
HEAD_WIDTH = 128
INNER = 16384
STATE_WIDTH = 16
DECAY_CHANNELS = 64
SPAN = 8
PICKED_BLOCKS = 4
BLOCK_TOKENS = 512
TOKEN_TOTAL = 16384
BLOCK_TOTAL = 32
NDOC = 64
DOCMAX = 4096
SCAN_HEAD_COUNT = 256


def log_uniform(key, shape, low, high):
    return jnp.exp(jax.random.uniform(key, shape, jnp.float32, jnp.log(low), jnp.log(high)))


def draw_queries(key, part):
    start_point = jnp.clip(jax.random.normal(jax.random.fold_in(key, 11), (TOKEN_TOTAL, QUERY_HEADS * HEAD_WIDTH), jnp.float32), -6.0, 6.0)
    return start_point.astype(jnp.bfloat16)


def draw_keys(key, part):
    start_point = jnp.clip(jax.random.normal(jax.random.fold_in(key, 12), (TOKEN_TOTAL, KEY_VALUE_HEADS * HEAD_WIDTH), jnp.float32), -6.0, 6.0)
    return start_point.astype(jnp.bfloat16)


def draw_block_plan(key, part):
    scores = jax.random.randint(jax.random.fold_in(key, 13), (BLOCK_TOTAL, SPAN - 1), 0, 1 << 20) * SPAN
    scores = scores + jnp.arange(SPAN - 1, dtype=jnp.int32)[None, :]
    scores = scores.at[0, SPAN - 2].set(-1)
    ranking = jnp.argsort(scores, axis=1)
    picked = (ranking[:, :PICKED_BLOCKS - 1] + 1).astype(jnp.int32)
    return jnp.concatenate([jnp.zeros((BLOCK_TOTAL, 1), jnp.int32), picked], axis=1)


def head_law(key):
    share = 0.5
    slow_heads = jax.random.uniform(jax.random.fold_in(key, 5301), (SCAN_HEAD_COUNT,), jnp.float32) < share
    rate = jnp.where(slow_heads, log_uniform(jax.random.fold_in(key, 5302), (SCAN_HEAD_COUNT,), 0.05, 0.09), log_uniform(jax.random.fold_in(key, 5303), (SCAN_HEAD_COUNT,), 0.5, 1.5))
    step_start_value = jnp.where(slow_heads, log_uniform(jax.random.fold_in(key, 5304), (SCAN_HEAD_COUNT,), 0.002, 0.004), log_uniform(jax.random.fold_in(key, 5305), (SCAN_HEAD_COUNT,), 0.02, 0.05))
    return (rate, step_start_value)


def draw_decay_rate(key, part):
    rate, step_start_value = head_law(key)
    return rate.astype(jnp.float32)


def draw_step_size(key, part):
    rate, step_start_value = head_law(key)
    coarse_scores = log_uniform(jax.random.fold_in(key, 5306), (TOKEN_TOTAL, SCAN_HEAD_COUNT), 0.5, 2.0)
    token_runs = jax.random.randint(jax.random.fold_in(key, 5307), (TOKEN_TOTAL,), 0, 4 * BLOCK_TOKENS) == 0
    value_result = step_start_value[None, :] * coarse_scores + 5.0 * token_runs.astype(jnp.float32)[:, None]
    return value_result.astype(jnp.bfloat16)


def draw_gate_input(key, part):
    channel_scale = 10.0 ** (jnp.arange(INNER, dtype=jnp.float32) / INNER)
    channel_scale = channel_scale * log_uniform(jax.random.fold_in(key, 21), (INNER,), 0.7, 1.4)
    row_scale = log_uniform(jax.random.fold_in(key, 22), (TOKEN_TOTAL, 1), 1.0, 10.0)
    start_point = jnp.clip(jax.random.normal(jax.random.fold_in(key, 24), (TOKEN_TOTAL, INNER), jnp.float32), -4.0, 4.0)
    return (start_point * channel_scale[None, :] * row_scale).astype(jnp.bfloat16)


def level_of(own_key, shape, pieces, smallest, high):
    level, own = 1.0, jax.random.fold_in(own_key, 6)
    for axis_at, blocks in pieces:
        steps = jnp.exp(jax.random.uniform(jax.random.fold_in(own, axis_at), (blocks,), jnp.float32, smallest / len(pieces), high / len(pieces)))
        level = level * jnp.repeat(steps, shape[axis_at] // blocks).reshape([-1 if axis == axis_at else 1 for axis in range(len(shape))])
    return level


def split_up(amount, total, limit, skew):
    loads = [(1 << 20) // math.isqrt(standing ** skew) + 1 for standing in range(2, amount + 1)]
    rest, given = total - limit - (amount - 1), [1] * (amount - 1)
    while rest > 0:
        movable = [i for i in range(amount - 1) if given[i] < limit]
        mass, budget = sum([loads[i] for i in movable]), rest
        for i in movable:
            more = min(limit - given[i], max(1, budget * loads[i] // mass), rest)
            given[i] = given[i] + more
            rest = rest - more
    return np.array([limit] + given)


def uneven(rng, number_of, total, bound, lean):
    if number_of == 2:
        one = jax.random.randint(rng, (), max(1, total - bound), min(bound, total - 1) + 1)
        return jnp.stack([one, total - one])
    sizes = jnp.asarray(split_up(number_of, total, bound, lean), jnp.int32)
    couples = (number_of - 1) // 2
    donor, taker = sizes[1:1 + 2 * couples:2], sizes[2:2 + 2 * couples:2]
    room = jnp.minimum(donor - 1, bound - taker)
    shifted = jax.random.randint(jax.random.fold_in(rng, 1), (couples,), 0, 1 << 20) % (room + 1)
    sizes = sizes.at[1:1 + 2 * couples:2].set(donor - shifted).at[2:2 + 2 * couples:2].set(taker + shifted)
    return sizes[jax.random.permutation(jax.random.fold_in(rng, 2), number_of)]


def scatter_about(rng, shape, deviation, limit, pieces=(), kind=jnp.bfloat16):
    drawn = jax.random.normal(rng, shape, jnp.float32) * deviation
    if len(pieces) > 0:
        drawn = level_of(rng, shape, pieces, -0.22, 0.18) * drawn
    return jnp.clip(drawn, min=-limit, max=limit).astype(kind)


def setup_inputs(seed: int = 0) -> dict:
    splits = jax.random.split(jax.random.key(seed), 14)
    queries = draw_queries(jax.random.fold_in(splits[13], 71), 0)
    keys = draw_keys(jax.random.fold_in(splits[13], 71), 0)
    values = scatter_about(splits[2], (TOKEN_TOTAL, KEY_VALUE_HEADS * HEAD_WIDTH), 1.0, 6.0, ((0, 32), (1, 4)))
    block_plan = draw_block_plan(jax.random.fold_in(splits[13], 71), 0)
    doc_lengths = uneven(splits[4], NDOC, TOKEN_TOTAL, DOCMAX, 2).astype(jnp.int32)
    scan_input = scatter_about(splits[5], (TOKEN_TOTAL, INNER), 1.0, 6.0, ((0, 32), (1, 4)))
    gate_input = draw_gate_input(jax.random.fold_in(splits[13], 71), 0)
    step_size = draw_step_size(jax.random.fold_in(splits[13], 71), 0)
    decay_rate = draw_decay_rate(jax.random.fold_in(splits[13], 71), 0)
    state_in = scatter_about(splits[9], (TOKEN_TOTAL, STATE_WIDTH), 1.0, 6.0, ((0, 32),))
    state_out = scatter_about(splits[10], (TOKEN_TOTAL, STATE_WIDTH), 1.0, 6.0, ((0, 32),))
    skip_gain = jnp.clip(0.5 + 1.0 * jax.random.uniform(splits[11], (SCAN_HEAD_COUNT,), jnp.float32) ** level_of(splits[11], (SCAN_HEAD_COUNT,), ((0, 4),), -0.2, 0.2), 0.5, 1.5)
    norm_gain = jnp.clip(1.0 + 0.1 * jax.random.normal(splits[12], (INNER,), jnp.float32), 0.5, 1.5)
    return dict(queries=queries, keys=keys, values=values, block_plan=block_plan, doc_lengths=doc_lengths, scan_input=scan_input, gate_input=gate_input, step_size=step_size, decay_rate=decay_rate, state_in=state_in, state_out=state_out, skip_gain=skip_gain, norm_gain=norm_gain)


def doc_index(positions, doc_lengths):
    doc_ends = jnp.cumsum(doc_lengths).astype(jnp.int32)
    return lax.optimization_barrier(jnp.sum((positions[:, None] >= doc_ends[None, :]).astype(jnp.int32), axis=1)).astype(jnp.int32)

def attention(queries, keys, values, block_plan, doc_lengths):
    query_group_width = QUERY_HEADS // KEY_VALUE_HEADS
    scale_factor = HEAD_WIDTH ** (-0.5)
    every_query = queries.reshape(BLOCK_TOTAL, BLOCK_TOKENS, KEY_VALUE_HEADS, query_group_width, HEAD_WIDTH)
    every_key = keys.reshape(BLOCK_TOTAL, BLOCK_TOKENS, KEY_VALUE_HEADS, HEAD_WIDTH)
    every_value = values.reshape(BLOCK_TOTAL, BLOCK_TOKENS, KEY_VALUE_HEADS, HEAD_WIDTH)
    offsets_row = jnp.arange(BLOCK_TOKENS, dtype=jnp.int32)

    def one_block(block_index):
        query_block = lax.dynamic_index_in_dim(every_query, block_index, 0, keepdims=False)
        chosen = block_index - block_plan[block_index]
        valid = chosen >= 0
        clamped_block = jnp.maximum(chosen, 0).astype(jnp.int32)
        picked_keys = every_key[clamped_block].reshape(PICKED_BLOCKS * BLOCK_TOKENS, KEY_VALUE_HEADS, HEAD_WIDTH)
        picked_values = every_value[clamped_block].reshape(PICKED_BLOCKS * BLOCK_TOKENS, KEY_VALUE_HEADS, HEAD_WIDTH)
        query_position = block_index * BLOCK_TOKENS + offsets_row
        key_position = (clamped_block[:, None] * BLOCK_TOKENS + offsets_row[None, :]).reshape(-1)
        key_valid = jnp.repeat(valid, BLOCK_TOKENS)
        allowed = key_valid[None, :] & (key_position[None, :] <= query_position[:, None])
        allowed = allowed & (doc_index(key_position, doc_lengths)[None, :] == doc_index(query_position, doc_lengths)[:, None])
        scores = jnp.einsum('tkgd,skd->kgts', query_block.astype(jnp.float32), picked_keys.astype(jnp.float32)) * scale_factor
        masked = jnp.where(allowed[None, None], scores, -1e+30)
        row_peak = lax.optimization_barrier(jnp.max(masked, axis=-1, keepdims=True))
        weights = jnp.where(allowed[None, None], jnp.exp(masked - row_peak), 0.0)
        denominator = lax.optimization_barrier(jnp.sum(weights, axis=-1))
        rounded = lax.optimization_barrier(weights.astype(jnp.bfloat16)).astype(jnp.float32)
        weighted = jnp.einsum('kgts,skd->tkgd', rounded, picked_values.astype(jnp.float32))
        result = weighted / jnp.transpose(denominator, (2, 0, 1))[..., None]
        return result.astype(jnp.bfloat16).reshape(BLOCK_TOKENS, QUERY_HEADS * HEAD_WIDTH)
    blocks_out = lax.map(one_block, jnp.arange(BLOCK_TOTAL, dtype=jnp.int32))
    return blocks_out.reshape(TOKEN_TOTAL, QUERY_HEADS * HEAD_WIDTH)

def selective_scan(scan_input, gate_input, step_size, decay_rate, state_in, state_out, skip_gain, norm_gain, doc_lengths):
    positions = jnp.arange(TOKEN_TOTAL, dtype=jnp.int32)
    token_doc = doc_index(positions, doc_lengths)
    first_flag = jnp.concatenate([jnp.ones((1,), dtype=bool), token_doc[1:] != token_doc[:-1]])

    def one_token(hidden_state, inputs):
        input_token, gate_token, step_token, in_token, out_token, first_token = inputs
        input_single = input_token.astype(jnp.float32).reshape(SCAN_HEAD_COUNT, DECAY_CHANNELS)
        step_float = step_token.astype(jnp.float32)
        decay = jnp.where(first_token, jnp.float32(0.0), jnp.exp(-decay_rate * step_float))
        drive_value = lax.optimization_barrier((step_float[:, None] * input_single).astype(jnp.bfloat16)).astype(jnp.float32)
        drive = drive_value[:, :, None] * in_token.astype(jnp.float32)[None, None, :]
        hidden_state = decay[:, None, None] * hidden_state + drive
        scan_y = lax.optimization_barrier(jnp.sum(hidden_state * out_token.astype(jnp.float32)[None, None, :], axis=-1)) + skip_gain[:, None] * input_single
        gated = scan_y.reshape(INNER) * jax.nn.silu(gate_token.astype(jnp.float32))
        result = gated * lax.rsqrt(jnp.mean(gated * gated) + 1e-05) * norm_gain
        return (hidden_state, result.astype(jnp.bfloat16))
    starting_state = jnp.zeros((SCAN_HEAD_COUNT, DECAY_CHANNELS, STATE_WIDTH), jnp.float32)
    _, mamba_out = lax.scan(one_token, starting_state, (scan_input, gate_input, step_size, state_in, state_out, first_flag))
    return mamba_out

def reference(queries, keys, values, block_plan, doc_lengths, scan_input, gate_input, step_size, decay_rate, state_in, state_out, skip_gain, norm_gain):
    attn_out = attention(queries, keys, values, block_plan, doc_lengths)
    mamba_out = selective_scan(scan_input, gate_input, step_size, decay_rate, state_in, state_out, skip_gain, norm_gain, doc_lengths)
    return (attn_out, mamba_out)
```

```python
import jax
import jax.numpy as jnp
from jax import lax
from jax.experimental import pallas as pl
from jax.experimental.pallas import tpu as pltpu
from jax.sharding import PartitionSpec as P

INNER = 16384
BIG = 16384.0
LOG2E=1.4426950408889634
def split_rows(a):
    high=a.astype(jnp.bfloat16)
    return jnp.concatenate([high,(a-high.astype(jnp.float32)).astype(jnp.bfloat16)],axis=0)
Q=128; NCH=4; CB=512; HB=CB//64
def local_kernel(sc_ref, meta_ref, x_ref, step_ref, stepT_ref, rrow_ref, rcol_ref, b_ref, bT_ref, c_ref, skip_ref,
                 y_ref, e_ref, ctdev_ref, ct, csT, wT, gm):
    i=pl.program_id(0)
    base=sc_ref[5]*512
    @pl.when(i==0)
    def _():
        r=lax.broadcasted_iota(jnp.int32,(Q,Q),0); cc=lax.broadcasted_iota(jnp.int32,(Q,Q),1)
        tril=jnp.where(cc<=r,1.0,0.0).astype(jnp.bfloat16)
        triu=jnp.where(r<=cc,1.0,0.0).astype(jnp.bfloat16)
        meta=meta_ref[...]
        prefix=jnp.zeros((1,64),jnp.float32)
        for k in range(NCH):
            sl=slice(k*Q,(k+1)*Q)
            cum=-dot(tril,step_ref[sl,:])*rrow_ref[...]
            dev=cum+prefix
            for ib in range(64//HB):
                ct[ib,sl,:]=cum[:,ib*HB:(ib+1)*HB]
                ctdev_ref[ib,sl,:]=dev[:,ib*HB:(ib+1)*HB]
            prefix=prefix+cum[Q-1:Q,:]
            st=stepT_ref[:,sl]
            cumT=-dot(st,triu)*rcol_ref[...]
            cs=cumT-jnp.log2(st.astype(jnp.float32))
            csT[:,sl]=cs
            pos=base+k*Q+lax.broadcasted_iota(jnp.int32,(64,Q),1)
            wT[:,sl]=jnp.where(pos>=sc_ref[10+k],jnp.exp2(cumT[:,Q-1:Q]-cs),0.0)
            oh=jnp.where(onehot_at(base+k*Q,Q,meta),1.0,0.0).astype(jnp.bfloat16)
            same=dotT(oh,oh)
            gm[k]=jnp.where((same>0.5)&(cc<=r),dotT(c_ref[sl,:],b_ref[sl,:]),0.0)
    lane=lax.broadcasted_iota(jnp.int32,(Q,128),1)
    first=lane<64
    H=[jnp.zeros((16,256),jnp.float32) for _ in range(HB//4)]
    T=[jnp.ones((1,256),jnp.float32) for _ in range(HB//4)]
    for k in range(NCH):
        sl=slice(k*Q,(k+1)*Q)
        ctk=ct[i,sl,:]
        csk=csT[pl.ds(pl.multiple_of(i*HB,HB),HB),sl]
        wk=wT[pl.ds(pl.multiple_of(i*HB,HB),HB),sl]
        gmk=gm[k]
        rowpos=base+k*Q+lax.broadcasted_iota(jnp.int32,(Q,128),0)
        enter=rowpos<sc_ref[6+k]
        flag=jnp.where(sc_ref[10+k]<base+k*Q,1.0,0.0)
        bTk=bT_ref[:,sl].astype(jnp.float32)
        cc2=jnp.concatenate([c_ref[sl,:],c_ref[sl,:]],axis=1)
        for qd in range(HB//4):
            Hq=H[qd]; ys=[]; es=[]; Rs=[]
            Yst=dot(cc2,split_rows(Hq))
            for pr in range(2):
                h0=qd*4+pr*2
                xp=x_ref[sl,h0*64:h0*64+128]
                z=jnp.zeros_like(xp)
                rhs=jnp.concatenate([jnp.where(first,xp,z),jnp.where(first,z,xp)],axis=0)
                Ms=[];Ts=[];cb=[]
                for u in range(2):
                    h=h0+u
                    ctb=jnp.broadcast_to(ctk[:,h:h+1],(Q,Q))
                    cb.append(ctb)
                    Ms.append((jnp.exp2(jnp.minimum(ctb-csk[h:h+1,:],3.0))*gmk).astype(jnp.bfloat16))
                    Ts.append(split_rows(bTk*wk[h:h+1,:]))
                lhs=jnp.concatenate([jnp.concatenate(Ms,axis=1),jnp.concatenate(Ts,axis=1)],axis=0)
                R=dot(lhs,rhs)
                e=jnp.exp2(jnp.where(first,cb[0],cb[1]))
                col=slice(h0*64,h0*64+128)
                y_ref[sl,col]=(R[:Q]+jnp.where(enter,e,0.0)*Yst[:,pr*128:(pr+1)*128]+skip_ref[0:1,col]*xp.astype(jnp.float32)).astype(y_ref.dtype)
                Rs.append(R[Q:Q+16]+R[Q+16:]); es.append(e[Q-1:Q,:]*flag)
            carry=jnp.concatenate(es,axis=1)
            H[qd]=carry*Hq+jnp.concatenate(Rs,axis=1)
            T[qd]=carry*T[qd]
    for qd in range(HB//4):
        e_ref[0:16,qd*256:(qd+1)*256]=H[qd]
        e_ref[16:24,qd*256:(qd+1)*256]=jnp.broadcast_to(T[qd],(8,256))

def local(sc,meta,x,step,stepT,rrow,rcol,b,bT,c,skip):
    full=lambda s: pl.BlockSpec(s,lambda i,_:(0,0))
    return pl.pallas_call(local_kernel,
        grid_spec=pltpu.PrefetchScalarGridSpec(num_scalar_prefetch=1,grid=(4096//CB,),
          in_specs=[full((8,128)),pl.BlockSpec((512,CB),lambda i,_:(0,i)),full((512,64)),full((64,512)),full((1,64)),full((64,1)),full((512,16)),full((16,512)),full((512,16)),pl.BlockSpec((1,CB),lambda i,_:(0,i))],
          out_specs=[pl.BlockSpec((512,CB),lambda i,_:(0,i)),pl.BlockSpec((24,CB),lambda i,_:(0,i)),pl.BlockSpec((64//HB,512,HB),lambda i,_:(0,0,0))],
          scratch_shapes=[pltpu.VMEM((64//HB,512,HB),jnp.float32),pltpu.VMEM((64,512),jnp.float32),pltpu.VMEM((64,512),jnp.float32),pltpu.VMEM((NCH,Q,Q),jnp.float32)]),
        out_shape=[jax.ShapeDtypeStruct((512,4096),jnp.bfloat16),jax.ShapeDtypeStruct((24,4096),jnp.float32),jax.ShapeDtypeStruct((64//HB,512,HB),jnp.float32)],
        compiler_params=pltpu.CompilerParams(vmem_limit_bytes=62000000),
        name="scan_local",
        cost_estimate=pl.CostEstimate(flops=10**6,bytes_accessed=10**4,transcendentals=0),
    )(sc,meta,x,step,stepT,rrow,rcol,b,bT,c,skip)

def gate_kernel(sc_ref,y_ref,g_ref,ct_ref,c_ref,h_ref,o_ref,sq_ref):
    i=pl.program_id(0)
    base=sc_ref[5]*512
    lane=lax.broadcasted_iota(jnp.int32,(Q,128),1)
    first=lane<64
    @pl.when(i==0)
    def _(): sq_ref[...]=jnp.zeros_like(sq_ref)
    for k in range(NCH):
        sl=slice(k*Q,(k+1)*Q)
        enter=base+k*Q+lax.broadcasted_iota(jnp.int32,(Q,128),0)<sc_ref[6]
        sq=sq_ref[sl,:]
        cc2=jnp.concatenate([c_ref[sl,:],c_ref[sl,:]],axis=1)
        ctk=ct_ref[sl,:]
        for w in range(CB//256):
            Y=dot(cc2,split_rows(h_ref[:,w*256:(w+1)*256]))
            for pr in range(2):
                h0=w*4+pr*2
                e=jnp.exp2(jnp.where(first,jnp.broadcast_to(ctk[:,h0:h0+1],(Q,128)),jnp.broadcast_to(ctk[:,h0+1:h0+2],(Q,128))))
                e=jnp.where(enter,e,0.0)
                col=slice(h0*64,h0*64+128)
                y=y_ref[sl,col].astype(jnp.float32)+e*Y[:,pr*128:(pr+1)*128]
                g=0.5*g_ref[sl,col].astype(jnp.float32)
                v=y*(g+g*jnp.tanh(g))
                sq=sq+v*v
                o_ref[sl,col]=v.astype(o_ref.dtype)
        sq_ref[sl,:]=sq

def gate(sc,y,g,ct,c,h):
    full=lambda s: pl.BlockSpec(s,lambda i,_:(0,0))
    blk=pl.BlockSpec((512,CB),lambda i,_:(0,i))
    return pl.pallas_call(gate_kernel,
        grid_spec=pltpu.PrefetchScalarGridSpec(num_scalar_prefetch=1,grid=(4096//CB,),
          in_specs=[blk,blk,pl.BlockSpec((None,512,HB),lambda i,_:(i,0,0)),full((512,16)),pl.BlockSpec((16,CB),lambda i,_:(0,i))],
          out_specs=[blk,full((512,128))]),
        out_shape=[jax.ShapeDtypeStruct((512,4096),jnp.bfloat16),jax.ShapeDtypeStruct((512,128),jnp.float32)],
        compiler_params=pltpu.CompilerParams(vmem_limit_bytes=62000000),
        name="scan_gate",
        cost_estimate=pl.CostEstimate(flops=10**6,bytes_accessed=10**4,transcendentals=0),
    )(sc,y,g,ct,c,h)

def dotT(a,b): return lax.dot_general(a,b,(((1,),(1,)),((),())),preferred_element_type=jnp.float32)
def dot(a,b): return lax.dot_general(a,b,(((1,),(0,)),((),())),preferred_element_type=jnp.float32)

def onehot_at(first, rows, meta):
    pos = first + lax.broadcasted_iota(jnp.int32,(rows,128),0)
    return (pos >= meta[0:1,:]) & (pos < meta[1:2,:])
TQ=256
def attn_kernel(sc_ref, meta_ref, q_ref, *rest):
    kv = rest[:9]; o_ref = rest[9]; kvbuf, ka, ve, ohq, s_a, s_b, cmask, sem = rest[10:]
    n_act = sc_ref[4]
    me = sc_ref[5]
    for j in range(4):
        off = sc_ref[j]
        @pl.when(j < n_act)
        def _():
            core = lax.rem(me,2)
            where_at = jnp.where(lax.rem(off,2)==0, off//2, 4+(off+1-core)//2)
            for k in range(9):
                @pl.when(where_at==k)
                def _(k=k):
                    pltpu.make_async_copy(kv[k], kvbuf.at[j], sem.at[j]).start()
    meta = meta_ref[...]
    ohq[...] = jnp.where(onehot_at(me*512,512,meta),1.0,0.0).astype(jnp.bfloat16)
    r = lax.broadcasted_iota(jnp.int32,(TQ,TQ),0); cc=lax.broadcasted_iota(jnp.int32,(TQ,TQ),1)
    cmask[...] = jnp.where(cc<=r, 0.0, -1e30)
    for j in range(4):
        @pl.when(j < n_act)
        def _():
            off = sc_ref[j]
            pltpu.make_async_copy(kv[0], kvbuf.at[j], sem.at[j]).wait()
            bias = jnp.where(onehot_at((me-off)*512,512,meta),0.0,-BIG).astype(jnp.bfloat16)
            for g in range(2):
                ka[g,j,:,0:128] = kvbuf[j,:,g*128:(g+1)*128]
                ka[g,j,:,128:256] = bias
                ve[g,j,:,0:128] = kvbuf[j,:,256+g*128:256+(g+1)*128]
                ve[g,j,:,128:256] = jnp.ones((512,128),jnp.bfloat16)
    c = jnp.float32(128**-0.5*1.4426950408889634)
    def variant(n):
        W=[TQ+512*(n-1), 512*n]
        def score(h,t,s_ref):
            g=h//8
            col=pl.multiple_of(h*128,128)
            qa = jnp.concatenate([q_ref[t*TQ:(t+1)*TQ,pl.ds(col,128)], ohq[t*TQ:(t+1)*TQ,:]],axis=1)
            at=0
            if t>0:
                s_ref[:,0:TQ]=dotT(qa,ka[g,0,0:TQ,:]); at=TQ
            s_ref[:,at:at+TQ]=dotT(qa,ka[g,0,t*TQ:(t+1)*TQ,:])+cmask[...]
            at+=TQ
            for j in range(1,n):
                s_ref[:,at:at+512]=dotT(qa,ka[g,j]); at+=512
        def soft(h,t,s_ref):
            g=h//8
            w=W[t]
            m=s_ref[:,0:128]
            for k in range(1,w//128): m=jnp.maximum(m,s_ref[:,k*128:(k+1)*128])
            mc=jnp.max(m,axis=1,keepdims=True)*c
            at=0; acc=None
            segs=[(0,0,(t+1)*TQ)]+[(j,0,512) for j in range(1,n)]
            for j,lo,hi in segs:
                p=jnp.exp2(s_ref[:,at:at+hi-lo]*c-mc).astype(jnp.bfloat16); at+=hi-lo
                a=dot(p,ve[g,j,lo:hi,:])
                acc = a if acc is None else acc+a
            col=pl.multiple_of(h*128,128)
            o_ref[t*TQ:(t+1)*TQ,pl.ds(col,128)]=(acc[:,:128]/acc[:,128:]).astype(jnp.bfloat16)
        score(0,0,s_a)
        def body(h,_):
            score(h,1,s_b)
            soft(h,0,s_a)
            hn=jnp.minimum(h+1,15)
            score(hn,0,s_a)
            soft(h,1,s_b)
            return 0
        lax.fori_loop(0,16,body,0)
    for n in range(1,5):
        @pl.when(n_act==n)
        def _(n=n): variant(n)

def attention(sc, meta, q, kvs):
    return pl.pallas_call(attn_kernel,
        grid_spec=pltpu.PrefetchScalarGridSpec(num_scalar_prefetch=1, grid=(1,),
            in_specs=[pl.BlockSpec((8,128),lambda h,s:(0,0)), pl.BlockSpec((512,2048),lambda h,s:(0,0))]+[pl.BlockSpec(memory_space=pl.ANY)]*9,
            out_specs=pl.BlockSpec((512,2048),lambda h,s:(0,0)),
            scratch_shapes=[pltpu.VMEM((4,512,512),jnp.bfloat16),pltpu.VMEM((2,4,512,256),jnp.bfloat16),pltpu.VMEM((2,4,512,256),jnp.bfloat16),pltpu.VMEM((512,128),jnp.bfloat16),
              pltpu.VMEM((TQ,2048),jnp.float32),pltpu.VMEM((TQ,2048),jnp.float32),pltpu.VMEM((TQ,TQ),jnp.float32),pltpu.SemaphoreType.DMA((4,))]),
        out_shape=jax.ShapeDtypeStruct((512,2048),jnp.bfloat16),
        compiler_params=pltpu.CompilerParams(vmem_limit_bytes=62000000),
        name="attention",
        cost_estimate=pl.CostEstimate(flops=10**6,bytes_accessed=10**4,transcendentals=0),
    )(sc,meta,q,*kvs)


def chip_pairs(move):
    return [
        (i, j)
        for i in range(32)
        for j in [move(i // 8, (i // 2) % 4, i % 2)]
        if j is not None
    ]


def spot(z, y, c):
    return (z * 4 + y % 4) * 2 + c if 0 <= z < 4 else None


def along_y(x, by):
    return lax.ppermute(x, "ctx", chip_pairs(lambda z, y, c: spot(z, y + by, c)))


def along_z(x):
    return lax.ppermute(x, "ctx", chip_pairs(lambda z, y, c: spot(z + 1, y, c)))


def swap_cores(x):
    return lax.ppermute(x, "ctx", [(i, i ^ 1) for i in range(32)])


def chips_back(x, by):
    return lax.ppermute(x, "ctx", [(i, i + 2 * by) for i in range(32 - 2 * by)])


def carry_state(state, core):
    half = state.shape[1] // 2
    left, right = state[:17, :half], state[:17, half:]
    mine = jnp.where(core == 0, left, right)
    got = swap_cores(jnp.where(core == 0, right, left))
    first = jnp.where(core == 0, mine, got)
    later = jnp.where(core == 0, got, mine)
    e0, t0 = first[:16], first[16:]
    e1, t1 = later[:16], later[16:]
    chip = jnp.concatenate([e1 + t1 * e0, t0 * t1], axis=0)
    parts = [chips_back(chip, by) for by in (1, 2, 3, 4)]
    held = parts[3][:16]
    for part in parts[2::-1]:
        held = part[:16] + part[16:] * held
    second = e0 + t0 * held
    keep = jnp.where(core == 0, held, second)
    got = swap_cores(jnp.where(core == 0, second, held))
    return jnp.concatenate(
        [jnp.where(core == 0, keep, got), jnp.where(core == 0, got, keep)], axis=1
    )


def shards(
    queries,
    keys,
    values,
    block_plan,
    doc_lengths,
    scan_input,
    gate_input,
    step_size,
    decay_rate,
    state_in,
    state_out,
    skip_gain,
    norm_gain,
):
    me = lax.axis_index("ctx")
    core = me % 2
    row = (me // 2) % 4
    kv = jnp.concatenate([keys, values], axis=1)
    above = along_z(kv)
    swapped = swap_cores(kv)

    n = jnp.arange(64, dtype=jnp.int32)
    ends = jnp.sum(jnp.where(n[:, None] <= n[None, :], doc_lengths[:, None], 0), axis=0)
    starts = ends - doc_lengths
    base = me * 512
    marks = base + 128 * jnp.arange(4, dtype=jnp.int32)
    before = marks - 1
    dend = jnp.max(
        jnp.where((starts[None] <= before[:, None]), ends[None], 0), axis=1
    )
    last = marks + 127
    dstart = jnp.max(jnp.where(starts[None] <= last[:, None], starts[None], 0), axis=1)
    open_doc = jnp.max(jnp.where(starts <= base, starts, 0))
    plan = lax.dynamic_index_in_dim(block_plan, me, 0, keepdims=False)
    live = (plan <= me) & (open_doc <= (me - plan) * 512 + 511)
    live = live | (jnp.arange(4) == 0)
    rank = jnp.sum(
        jnp.where(jnp.arange(4)[:, None] < jnp.arange(4)[None, :], live[:, None], False), axis=0
    )
    order = jnp.sum(
        jnp.where((rank[None] == jnp.arange(4)[:, None]) & live[None], plan[None], 0), axis=1
    )
    sc = jnp.concatenate(
        [order, jnp.sum(live)[None], me[None], dend, dstart, jnp.zeros((2,), jnp.int32)]
    ).astype(jnp.int32)
    far = jnp.full((64,), 1 << 30, jnp.int32)
    meta = jnp.stack([jnp.concatenate([starts, far]), jnp.concatenate([ends, far])])
    meta = jnp.concatenate([meta, jnp.zeros((6, 128), jnp.int32)])

    rate = decay_rate * LOG2E
    y, state, reach = local(
        sc,
        meta,
        scan_input,
        step_size,
        step_size.T,
        rate[None],
        rate[:, None],
        state_in,
        state_in.T,
        state_out,
        jnp.repeat(skip_gain, 64)[None],
    )
    state, above = lax.optimization_barrier((state, above))
    same = {
        by: along_y(jnp.where(row + by < 4, kv, above), by) for by in (1, 3, 2)
    }
    incoming = carry_state(state, core)
    gated, squares = gate(sc, y, gate_input, reach, state_out, incoming)
    squares, near, low, far_one, above = lax.optimization_barrier(
        (jnp.sum(squares, axis=1), same[1], same[3], same[2], above)
    )
    same = {0: kv, 1: near, 2: far_one, 3: low}
    other = [swapped] + [swap_cores(same[by]) for by in (1, 2, 3)] + [swap_cores(above)]
    squares = lax.psum(squares, "tp")

    blocks = [same[k] for k in range(4)] + [other[k] for k in range(5)]
    attn_out = attention(sc, meta, queries, blocks)
    scale = lax.rsqrt(squares / INNER + 1e-05)
    mamba_out = (gated.astype(jnp.float32) * scale[:, None] * norm_gain[None, :]).astype(
        jnp.bfloat16
    )
    return (attn_out, mamba_out)


def solution(mesh):
    in_specs = (
        P("ctx", "tp"),
        P("ctx", "tp"),
        P("ctx", "tp"),
        P(),
        P(),
        P("ctx", "tp"),
        P("ctx", "tp"),
        P("ctx", "tp"),
        P("tp"),
        P("ctx", None),
        P("ctx", None),
        P("tp"),
        P("tp"),
    )
    out_specs = (P("ctx", "tp"), P("ctx", "tp"))
    return jax.shard_map(shards, mesh=mesh, in_specs=in_specs, out_specs=out_specs, check_vma=False)
```

```python
import jax
import jax.numpy as jnp
from jax import lax
from jax.experimental import pallas as pl
from jax.experimental.pallas import tpu as pltpu
from jax.sharding import PartitionSpec as P

INNER = 16384
BIG = 16384.0
LOG2E = 1.4426950408889634
Q = 128
NCH = 4
TQ = 256
PARAMS = pltpu.CompilerParams(vmem_limit_bytes=62000000)
SMALL = pl.CostEstimate(flops=10**6, bytes_accessed=10**4, transcendentals=0)


def dot(a, b):
    return lax.dot_general(a, b, (((1,), (0,)), ((), ())), preferred_element_type=jnp.float32)


def dot_t(a, b):
    return lax.dot_general(a, b, (((1,), (1,)), ((), ())), preferred_element_type=jnp.float32)


def split_rows(a):
    high = a.astype(jnp.bfloat16)
    return jnp.concatenate([high, (a - high.astype(jnp.float32)).astype(jnp.bfloat16)], axis=0)


def eye_like():
    r = lax.broadcasted_iota(jnp.int32, (Q, Q), 0)
    c = lax.broadcasted_iota(jnp.int32, (Q, Q), 1)
    return r, c


def doc_rows(len_ref):
    lane = lax.broadcasted_iota(jnp.int32, (8, 128), 1)
    far = jnp.full((8, 128), 1 << 30, jnp.int32)

    def one(d, held):
        end, starts, ends = held
        later = end + len_ref[d]
        return later, jnp.where(lane == d, end, starts), jnp.where(lane == d, later, ends)

    _, starts, ends = lax.fori_loop(0, 64, one, (jnp.int32(0), far, far), unroll=8)
    return starts[0:1], ends[0:1]


def last_doc(len_ref, position):
    def one(d, held):
        at, start, end = held
        later = at + len_ref[d]
        inside = at <= position
        return later, jnp.where(inside, at, start), jnp.where(inside, later, end)

    _, start, end = lax.fori_loop(0, 64, one, (jnp.int32(0), jnp.int32(0), jnp.int32(0)), unroll=8)
    return start, end


def one_hot(first, rows, starts, ends):
    pos = first + lax.broadcasted_iota(jnp.int32, (rows, 128), 0)
    return (pos >= starts) & (pos < ends)


def row_to_column(row):
    return jnp.broadcast_to(row, (128, 128)).T


def cumulate(step_t, rate_row):
    r, c = eye_like()
    tril = jnp.where(c <= r, 1.0, 0.0).astype(jnp.bfloat16)
    return -dot_t(tril, step_t) * rate_row


def local_kernel(
    len_ref, me_ref, x_ref, step_ref, rate_ref, b_ref, c_ref, skip_ref, y_ref, e_ref, state,
):
    i = pl.program_id(0)
    base = me_ref[0] * 512
    first = base + i * Q

    @pl.when(i == 0)
    def _():
        state[0:16, :] = jnp.zeros((16, 4096), jnp.float32)
        state[16:24, :] = jnp.ones((8, 4096), jnp.float32)

    r, c = eye_like()
    eye = jnp.where(c == r, 1.0, 0.0).astype(jnp.bfloat16)
    triu = jnp.where(r <= c, 1.0, 0.0).astype(jnp.bfloat16)
    starts, ends = doc_rows(len_ref)
    rate_row = rate_ref[...] * LOG2E
    rate_col = jnp.sum(
        jnp.where(
            lax.broadcasted_iota(jnp.int32, (64, 64), 0)
            == lax.broadcasted_iota(jnp.int32, (64, 64), 1),
            rate_row,
            0.0,
        ),
        axis=1,
        keepdims=True,
    )
    _, end_before = last_doc(len_ref, first - 1)
    start_last, _ = last_doc(len_ref, first + Q - 1)
    st = step_ref[...]
    ct = cumulate(st, rate_row)
    cum_t = -dot(st, triu) * rate_col
    cs = cum_t - jnp.log2(st.astype(jnp.float32))
    pos = first + lax.broadcasted_iota(jnp.int32, (64, Q), 1)
    w_t = jnp.where(pos >= start_last, jnp.exp2(cum_t[:, Q - 1 : Q] - cs), 0.0)
    oh = jnp.where(one_hot(first, Q, starts, ends), 1.0, 0.0).astype(jnp.bfloat16)
    c_rows = dot_t(eye, c_ref[...]).astype(jnp.bfloat16)
    cc2 = jnp.concatenate([c_rows, c_rows], axis=1)
    gm = jnp.where((dot_t(oh, oh) > 0.5) & (c <= r), dot(c_rows, b_ref[...]), 0.0)
    b_k = b_ref[...].astype(jnp.float32)
    low = lax.broadcasted_iota(jnp.int32, (Q, 128), 1) < 64
    low_row = low[0:1]
    enter = first + lax.broadcasted_iota(jnp.int32, (Q, 128), 0) < end_before
    flag = jnp.where(start_last < first, 1.0, 0.0)
    for quad in range(16):
        four = slice(quad * 256, (quad + 1) * 256)
        held = state[0:16, four]
        from_state = dot(cc2, split_rows(held))
        added, carries = [], []
        for pair in range(2):
            h0 = quad * 4 + pair * 2
            col = slice(h0 * 64, h0 * 64 + 128)
            xp = x_ref[:, col]
            zero = jnp.zeros_like(xp)
            rhs = jnp.concatenate([jnp.where(low, xp, zero), jnp.where(low, zero, xp)], axis=0)
            mix, tail, cb = [], [], []
            for h in (h0, h0 + 1):
                c_b = jnp.broadcast_to(ct[:, h : h + 1], (Q, Q))
                cb.append(c_b)
                gap = jnp.minimum(c_b - cs[h : h + 1, :], 3.0)
                mix.append((jnp.exp2(gap) * gm).astype(jnp.bfloat16))
                tail.append(split_rows(b_k * w_t[h : h + 1, :]))
            lhs = jnp.concatenate(
                [jnp.concatenate(mix, axis=1), jnp.concatenate(tail, axis=1)], axis=0
            )
            res = dot(lhs, rhs)
            e = jnp.exp2(jnp.where(low, cb[0], cb[1]))
            skip = jnp.where(low_row, skip_ref[h0], skip_ref[h0 + 1])
            y_ref[:, col] = (
                res[:Q]
                + jnp.where(enter, e, 0.0) * from_state[:, pair * 128 : (pair + 1) * 128]
                + skip * xp.astype(jnp.float32)
            ).astype(y_ref.dtype)
            added.append(res[Q : Q + 16] + res[Q + 16 :])
            carries.append(e[Q - 1 : Q, :] * flag)
        carry = jnp.concatenate(carries, axis=1)
        state[0:16, four] = carry * held + jnp.concatenate(added, axis=1)
        state[16:17, four] = carry * state[16:17, four]

    @pl.when(i == NCH - 1)
    def _():
        e_ref[...] = state[0:17, :]


def whole(shape):
    return pl.BlockSpec(shape, lambda *_: (0,) * len(shape))


def smem():
    return pl.BlockSpec(memory_space=pltpu.SMEM)


def tokens(width):
    return pl.BlockSpec((Q, width), lambda i: (i, 0))


def across(rows):
    return pl.BlockSpec((rows, Q), lambda i: (0, i))


def local(doc_lengths, me, x, step_t, rate, b_t, c_t, skip):
    return pl.pallas_call(
        local_kernel,
        grid=(NCH,),
        in_specs=[
            smem(), smem(), tokens(4096), across(64), whole((1, 64)), across(16), across(16), smem(),
        ],
        out_specs=[tokens(4096), whole((17, 4096))],
        scratch_shapes=[pltpu.VMEM((24, 4096), jnp.float32)],
        out_shape=[
            jax.ShapeDtypeStruct((512, 4096), jnp.bfloat16),
            jax.ShapeDtypeStruct((17, 4096), jnp.float32),
        ],
        compiler_params=PARAMS,
        cost_estimate=SMALL,
        name="scan_local",
    )(doc_lengths, me, x, step_t, rate, b_t, c_t, skip)


def gate_kernel(
    len_ref, me_ref, y_ref, g_ref, step_ref, rate_ref, c_ref, h_ref, o_ref, row_ref, prefix,
):
    i = pl.program_id(0)
    base = me_ref[0] * 512

    @pl.when(i == 0)
    def _():
        prefix[...] = jnp.zeros_like(prefix)

    r, c = eye_like()
    eye = jnp.where(c == r, 1.0, 0.0).astype(jnp.bfloat16)
    _, end_before = last_doc(len_ref, base - 1)
    ct = cumulate(step_ref[...], rate_ref[...] * LOG2E) + prefix[0:1, :]
    prefix[0:1, :] = ct[Q - 1 : Q, :]
    c_rows = dot_t(eye, c_ref[...]).astype(jnp.bfloat16)
    cc2 = jnp.concatenate([c_rows, c_rows], axis=1)
    low = lax.broadcasted_iota(jnp.int32, (Q, 128), 1) < 64
    enter = base + i * Q + lax.broadcasted_iota(jnp.int32, (Q, 128), 0) < end_before
    sq = jnp.zeros((Q, 128), jnp.float32)
    for w in range(16):
        from_state = dot(cc2, split_rows(h_ref[:, w * 256 : (w + 1) * 256]))
        for pair in range(2):
            h0 = w * 4 + pair * 2
            col = slice(h0 * 64, h0 * 64 + 128)
            e = jnp.exp2(
                jnp.where(
                    low,
                    jnp.broadcast_to(ct[:, h0 : h0 + 1], (Q, 128)),
                    jnp.broadcast_to(ct[:, h0 + 1 : h0 + 2], (Q, 128)),
                )
            )
            y = y_ref[:, col].astype(jnp.float32) + jnp.where(enter, e, 0.0) * (
                from_state[:, pair * 128 : (pair + 1) * 128]
            )
            g = 0.5 * g_ref[:, col].astype(jnp.float32)
            v = y * (g + g * jnp.tanh(g))
            sq = sq + v * v
            o_ref[:, col] = v.astype(o_ref.dtype)
    row_ref[...] = jnp.sum(sq.T, axis=0, keepdims=True)


def gate(doc_lengths, me, y, g, step_t, rate, c_t, h):
    return pl.pallas_call(
        gate_kernel,
        grid=(NCH,),
        in_specs=[
            smem(), smem(), tokens(4096), tokens(4096), across(64), whole((1, 64)), across(16),
            whole((16, 4096)),
        ],
        out_specs=[tokens(4096), across(1)],
        scratch_shapes=[pltpu.VMEM((8, 64), jnp.float32)],
        out_shape=[
            jax.ShapeDtypeStruct((512, 4096), jnp.bfloat16),
            jax.ShapeDtypeStruct((1, 512), jnp.float32),
        ],
        compiler_params=PARAMS,
        cost_estimate=SMALL,
        name="scan_gate",
    )(doc_lengths, me, y, g, step_t, rate, c_t, h)


NB = 128


def norm_kernel(v_ref, s0, s1, s2, s3, gain_ref, o_ref):
    row = lax.rsqrt((s0[...] + s1[...] + s2[...] + s3[...]) / INNER + 1e-05)
    factor = row_to_column(row)
    for w in range(4096 // 128):
        col = slice(w * 128, (w + 1) * 128)
        o_ref[:, col] = (v_ref[:, col].astype(jnp.float32) * factor * gain_ref[:, col]).astype(
            o_ref.dtype
        )


def norm(v, sums, gain):
    rows = pl.BlockSpec((NB, 4096), lambda i: (i, 0))
    return pl.pallas_call(
        norm_kernel,
        grid=(512 // NB,),
        in_specs=[rows] + [pl.BlockSpec((1, NB), lambda i: (0, i))] * 4 + [whole((1, 4096))],
        out_specs=rows,
        out_shape=jax.ShapeDtypeStruct((512, 4096), jnp.bfloat16),
        compiler_params=pltpu.CompilerParams(vmem_limit_bytes=16 * 2**20),
        cost_estimate=SMALL,
        name="norm",
    )(v, *sums, gain)


def pack_kernel(k_ref, v_ref, o_ref):
    o_ref[:, 0:256] = k_ref[...]
    o_ref[:, 256:512] = v_ref[...]


def pack(keys, values):
    return pl.pallas_call(
        pack_kernel,
        out_shape=jax.ShapeDtypeStruct((512, 512), jnp.bfloat16),
        compiler_params=pltpu.CompilerParams(vmem_limit_bytes=8 * 2**20),
        cost_estimate=SMALL,
        name="pack",
    )(keys, values)


def attention_kernel(
    len_ref, plan_ref, me_ref, q_hbm, *rest
):
    kv = rest[:9]
    o_hbm, q_ref, o_ref, kv_buf, ka, ve, ohq, s_a, s_b, causal, order, sem = rest[9:]
    bring = pltpu.make_async_copy(q_hbm, q_ref, sem.at[4])
    bring.start()
    me = me_ref[0]
    core = lax.rem(me, 2)
    open_doc, _ = last_doc(len_ref, me * 512)
    order[0] = 0
    n_act = jnp.int32(1)
    for m in range(1, 4):
        off = plan_ref[m, me]
        order[n_act] = off
        n_act = n_act + jnp.where((off <= me) & (open_doc <= (me - off) * 512 + 511), 1, 0)
    for j in range(4):

        @pl.when(j < n_act)
        def _(j=j):
            off = order[j]
            source = jnp.where(lax.rem(off, 2) == 0, off // 2, 4 + (off + 1 - core) // 2)
            for k in range(9):

                @pl.when(source == k)
                def _(k=k):
                    pltpu.make_async_copy(kv[k], kv_buf.at[j], sem.at[j]).start()

    starts, ends = doc_rows(len_ref)
    ohq[...] = jnp.where(one_hot(me * 512, 512, starts, ends), 1.0, 0.0).astype(jnp.bfloat16)
    r = lax.broadcasted_iota(jnp.int32, (TQ, TQ), 0)
    c = lax.broadcasted_iota(jnp.int32, (TQ, TQ), 1)
    causal[...] = jnp.where(c <= r, 0.0, -1e30)
    for j in range(4):

        @pl.when(j < n_act)
        def _(j=j):
            pltpu.make_async_copy(kv[0], kv_buf.at[j], sem.at[j]).wait()
            same = one_hot((me - order[j]) * 512, 512, starts, ends)
            bias = jnp.where(same, 0.0, -BIG).astype(jnp.bfloat16)
            for g in range(2):
                ka[g, j, :, 0:128] = kv_buf[j, :, g * 128 : (g + 1) * 128]
                ka[g, j, :, 128:256] = bias
                ve[g, j, :, 0:128] = kv_buf[j, :, 256 + g * 128 : 256 + (g + 1) * 128]
                ve[g, j, :, 128:256] = jnp.ones((512, 128), jnp.bfloat16)

    bring.wait()
    factor = jnp.float32(128**-0.5 * LOG2E)

    def variant(n):
        def score(h, t, s_ref):
            g = h // 8
            col = pl.multiple_of(h * 128, 128)
            own = slice(t * TQ, (t + 1) * TQ)
            qa = jnp.concatenate([q_ref[own, pl.ds(col, 128)], ohq[own, :]], axis=1)
            at = 0
            if t > 0:
                s_ref[:, 0:TQ] = dot_t(qa, ka[g, 0, 0:TQ, :])
                at = TQ
            s_ref[:, at : at + TQ] = dot_t(qa, ka[g, 0, own, :]) + causal[...]
            at += TQ
            for j in range(1, n):
                s_ref[:, at : at + 512] = dot_t(qa, ka[g, j])
                at += 512

        def soft(h, t, s_ref):
            g = h // 8
            width = (t + 1) * TQ + 512 * (n - 1)
            peak = s_ref[:, 0:128]
            for k in range(1, width // 128):
                peak = jnp.maximum(peak, s_ref[:, k * 128 : (k + 1) * 128])
            peak = jnp.max(peak, axis=1, keepdims=True) * factor
            at = 0
            total = None
            for j, rows in [(0, (t + 1) * TQ)] + [(j, 512) for j in range(1, n)]:
                w = jnp.exp2(s_ref[:, at : at + rows] * factor - peak).astype(jnp.bfloat16)
                at += rows
                part = dot(w, ve[g, j, 0:rows, :])
                total = part if total is None else total + part
            col = pl.multiple_of(h * 128, 128)
            o_ref[t * TQ : (t + 1) * TQ, pl.ds(col, 128)] = (
                total[:, :128] / total[:, 128:]
            ).astype(jnp.bfloat16)

        score(0, 0, s_a)

        def body(h, _):
            score(h, 1, s_b)
            soft(h, 0, s_a)
            score(jnp.minimum(h + 1, 15), 0, s_a)
            soft(h, 1, s_b)
            return 0

        lax.fori_loop(0, 8, body, 0)
        halves[0].start()
        lax.fori_loop(8, 16, body, 0)
        halves[1].start()

    halves = [
        pltpu.make_async_copy(o_ref.at[:, part], o_hbm.at[:, part], sem.at[5 + p])
        for p, part in enumerate((slice(0, 1024), slice(1024, 2048)))
    ]
    for n in range(1, 5):

        @pl.when(n_act == n)
        def _(n=n):
            variant(n)

    halves[0].wait()
    halves[1].wait()


def attention(doc_lengths, plan, me, q, blocks):
    return pl.pallas_call(
        attention_kernel,
        in_specs=[smem(), smem(), smem()] + [pl.BlockSpec(memory_space=pl.ANY)] * 10,
        out_specs=pl.BlockSpec(memory_space=pl.ANY),
        scratch_shapes=[
            pltpu.VMEM((512, 2048), jnp.bfloat16),
            pltpu.VMEM((512, 2048), jnp.bfloat16),
            pltpu.VMEM((4, 512, 512), jnp.bfloat16),
            pltpu.VMEM((2, 4, 512, 256), jnp.bfloat16),
            pltpu.VMEM((2, 4, 512, 256), jnp.bfloat16),
            pltpu.VMEM((512, 128), jnp.bfloat16),
            pltpu.VMEM((TQ, 2048), jnp.float32),
            pltpu.VMEM((TQ, 2048), jnp.float32),
            pltpu.VMEM((TQ, TQ), jnp.float32),
            pltpu.SMEM((4,), jnp.int32),
            pltpu.SemaphoreType.DMA((7,)),
        ],
        out_shape=jax.ShapeDtypeStruct((512, 2048), jnp.bfloat16),
        compiler_params=PARAMS,
        cost_estimate=pl.CostEstimate(flops=3 * 10**10, bytes_accessed=10**7, transcendentals=0),
        name="attention",
    )(doc_lengths, plan, me, q, *blocks)


def chip_pairs(move):
    return [
        (i, j)
        for i in range(32)
        for j in [move(i // 8, (i // 2) % 4, i % 2)]
        if j is not None
    ]


def spot(z, y, c):
    return (z * 4 + y % 4) * 2 + c if 0 <= z < 4 else None


def along_y(x, by):
    return lax.ppermute(x, "ctx", chip_pairs(lambda z, y, c: spot(z, y + by, c)))


def along_z(x):
    return lax.ppermute(x, "ctx", chip_pairs(lambda z, y, c: spot(z + 1, y, c)))


def swap_cores(x):
    return lax.ppermute(x, "ctx", [(i, i ^ 1) for i in range(32)])


def chips_back(x, by):
    return lax.ppermute(x, "ctx", [(i, i + 2 * by) for i in range(32 - 2 * by)])


def carry_state(state, core):
    half = state.shape[1] // 2
    left, right = state[:17, :half], state[:17, half:]
    mine = jnp.where(core == 0, left, right)
    got = swap_cores(jnp.where(core == 0, right, left))
    first = jnp.where(core == 0, mine, got)
    later = jnp.where(core == 0, got, mine)
    e0, t0 = first[:16], first[16:]
    e1, t1 = later[:16], later[16:]
    chip = jnp.concatenate([e1 + t1 * e0, t0 * t1], axis=0)
    parts = [chips_back(chip, by) for by in (1, 2, 3, 4)]
    held = parts[3][:16]
    for part in parts[2::-1]:
        held = part[:16] + part[16:] * held
    second = e0 + t0 * held
    keep = jnp.where(core == 0, held, second)
    got = swap_cores(jnp.where(core == 0, second, held))
    return jnp.concatenate(
        [jnp.where(core == 0, keep, got), jnp.where(core == 0, got, keep)], axis=1
    )


def shards(
    queries,
    keys,
    values,
    block_plan,
    doc_lengths,
    scan_input,
    gate_input,
    step_size,
    decay_rate,
    state_in,
    state_out,
    skip_gain,
    norm_gain,
):
    me = lax.axis_index("ctx")
    core = me % 2
    row = (me // 2) % 4
    kv = pack(keys, values)
    above = along_z(kv)
    swapped = swap_cores(kv)
    me1 = me.reshape(1)
    step_t = step_size.T
    rate = decay_rate[None]
    c_t = state_out.T
    y, state = local(
        doc_lengths, me1, scan_input, step_t, rate, state_in.T, c_t, skip_gain
    )
    state, above = lax.optimization_barrier((state, above))
    same = {by: along_y(jnp.where(row + by < 4, kv, above), by) for by in (1, 3, 2)}
    incoming = carry_state(state, core)
    gated, squares = gate(
        doc_lengths, me1, y, gate_input, step_t, rate, c_t, incoming
    )
    sums = [squares] + [
        lax.ppermute(squares, "tp", [(i, (i + by) % 4) for i in range(4)]) for by in (1, 3, 2)
    ]
    sums, near, low, far_one, above = lax.optimization_barrier(
        (sums, same[1], same[3], same[2], above)
    )
    blocks = [kv, near, far_one, low, swapped]
    blocks += [swap_cores(b) for b in (near, far_one, low, above)]
    attn_out = attention(doc_lengths, block_plan.T, me1, queries, blocks)
    gated, attn_out = lax.optimization_barrier((gated, attn_out))
    mamba_out = norm(gated, sums, norm_gain[None])
    return (attn_out, mamba_out)


def solution(mesh):
    in_specs = (
        P("ctx", "tp"),
        P("ctx", "tp"),
        P("ctx", "tp"),
        P(),
        P(),
        P("ctx", "tp"),
        P("ctx", "tp"),
        P("ctx", "tp"),
        P("tp"),
        P("ctx", None),
        P("ctx", None),
        P("tp"),
        P("tp"),
    )
    out_specs = (P("ctx", "tp"), P("ctx", "tp"))
    return jax.shard_map(shards, mesh=mesh, in_specs=in_specs, out_specs=out_specs, check_vma=False)
```

```python
import jax
import jax.numpy as jnp
from jax import lax
from jax.experimental import pallas as pl
from jax.experimental.pallas import tpu as pltpu
from jax.sharding import PartitionSpec as P

INNER = 16384
BIG = 16384.0
LOG2E = 1.4426950408889634
Q = 128
NCH = 4
TQ = 256
PARAMS = pltpu.CompilerParams(vmem_limit_bytes=62000000)
SMALL = pl.CostEstimate(flops=10**6, bytes_accessed=10**4, transcendentals=0)


def dot(a, b):
    return lax.dot_general(a, b, (((1,), (0,)), ((), ())), preferred_element_type=jnp.float32)


def dot_t(a, b):
    return lax.dot_general(a, b, (((1,), (1,)), ((), ())), preferred_element_type=jnp.float32)


def split_rows(a):
    high = a.astype(jnp.bfloat16)
    return jnp.concatenate([high, (a - high.astype(jnp.float32)).astype(jnp.bfloat16)], axis=0)


def eye_like():
    r = lax.broadcasted_iota(jnp.int32, (Q, Q), 0)
    c = lax.broadcasted_iota(jnp.int32, (Q, Q), 1)
    return r, c


def doc_rows(len_ref):
    lane = lax.broadcasted_iota(jnp.int32, (8, 128), 1)
    far = jnp.full((8, 128), 1 << 30, jnp.int32)

    def one(d, held):
        end, starts, ends = held
        later = end + len_ref[d]
        return later, jnp.where(lane == d, end, starts), jnp.where(lane == d, later, ends)

    _, starts, ends = lax.fori_loop(0, 64, one, (jnp.int32(0), far, far), unroll=8)
    return starts[0:1], ends[0:1]


def last_doc(len_ref, position):
    def one(d, held):
        at, start, end = held
        later = at + len_ref[d]
        inside = at <= position
        return later, jnp.where(inside, at, start), jnp.where(inside, later, end)

    _, start, end = lax.fori_loop(0, 64, one, (jnp.int32(0), jnp.int32(0), jnp.int32(0)), unroll=8)
    return start, end


def one_hot(first, rows, starts, ends):
    pos = first + lax.broadcasted_iota(jnp.int32, (rows, 128), 0)
    return (pos >= starts) & (pos < ends)


def row_to_column(row):
    return jnp.broadcast_to(row, (128, 128)).T


def cumulate(step_t, rate_row):
    r, c = eye_like()
    tril = jnp.where(c <= r, 1.0, 0.0).astype(jnp.bfloat16)
    return -dot_t(tril, step_t) * rate_row


def local_kernel(
    len_ref, me_ref, x_ref, step_ref, rate_ref, b_ref, c_ref, skip_ref, y_ref, e_ref, state,
):
    i = pl.program_id(0)
    base = me_ref[0] * 512
    first = base + i * Q

    @pl.when(i == 0)
    def _():
        state[0:16, :] = jnp.zeros((16, 4096), jnp.float32)
        state[16:24, :] = jnp.ones((8, 4096), jnp.float32)

    r, c = eye_like()
    eye = jnp.where(c == r, 1.0, 0.0).astype(jnp.bfloat16)
    triu = jnp.where(r <= c, 1.0, 0.0).astype(jnp.bfloat16)
    starts, ends = doc_rows(len_ref)
    rate_row = rate_ref[...] * LOG2E
    rate_col = jnp.sum(
        jnp.where(
            lax.broadcasted_iota(jnp.int32, (64, 64), 0)
            == lax.broadcasted_iota(jnp.int32, (64, 64), 1),
            rate_row,
            0.0,
        ),
        axis=1,
        keepdims=True,
    )
    _, end_before = last_doc(len_ref, first - 1)
    start_last, _ = last_doc(len_ref, first + Q - 1)
    st = step_ref[...]
    ct = cumulate(st, rate_row)
    cum_t = -dot(st, triu) * rate_col
    cs = cum_t - jnp.log2(st.astype(jnp.float32))
    pos = first + lax.broadcasted_iota(jnp.int32, (64, Q), 1)
    w_t = jnp.where(pos >= start_last, jnp.exp2(cum_t[:, Q - 1 : Q] - cs), 0.0)
    oh = jnp.where(one_hot(first, Q, starts, ends), 1.0, 0.0).astype(jnp.bfloat16)
    c_rows = dot_t(eye, c_ref[...]).astype(jnp.bfloat16)
    cc2 = jnp.concatenate([c_rows, c_rows], axis=1)
    gm = jnp.where((dot_t(oh, oh) > 0.5) & (c <= r), dot(c_rows, b_ref[...]), 0.0)
    b_k = b_ref[...].astype(jnp.float32)
    low = lax.broadcasted_iota(jnp.int32, (Q, 128), 1) < 64
    low_row = low[0:1]
    enter = first + lax.broadcasted_iota(jnp.int32, (Q, 128), 0) < end_before
    flag = jnp.where(start_last < first, 1.0, 0.0)
    for quad in range(16):
        four = slice(quad * 256, (quad + 1) * 256)
        held = state[0:16, four]
        from_state = dot(cc2, split_rows(held))
        added, carries = [], []
        for pair in range(2):
            h0 = quad * 4 + pair * 2
            col = slice(h0 * 64, h0 * 64 + 128)
            xp = x_ref[:, col]
            zero = jnp.zeros_like(xp)
            rhs = jnp.concatenate([jnp.where(low, xp, zero), jnp.where(low, zero, xp)], axis=0)
            mix, tail, cb = [], [], []
            for h in (h0, h0 + 1):
                c_b = jnp.broadcast_to(ct[:, h : h + 1], (Q, Q))
                cb.append(c_b)
                gap = jnp.minimum(c_b - cs[h : h + 1, :], 3.0)
                mix.append((jnp.exp2(gap) * gm).astype(jnp.bfloat16))
                tail.append(split_rows(b_k * w_t[h : h + 1, :]))
            lhs = jnp.concatenate(
                [jnp.concatenate(mix, axis=1), jnp.concatenate(tail, axis=1)], axis=0
            )
            res = dot(lhs, rhs)
            e = jnp.exp2(jnp.where(low, cb[0], cb[1]))
            skip = jnp.where(low_row, skip_ref[h0], skip_ref[h0 + 1])
            y_ref[:, col] = (
                res[:Q]
                + jnp.where(enter, e, 0.0) * from_state[:, pair * 128 : (pair + 1) * 128]
                + skip * xp.astype(jnp.float32)
            ).astype(y_ref.dtype)
            added.append(res[Q : Q + 16] + res[Q + 16 :])
            carries.append(e[Q - 1 : Q, :] * flag)
        carry = jnp.concatenate(carries, axis=1)
        state[0:16, four] = carry * held + jnp.concatenate(added, axis=1)
        state[16:17, four] = carry * state[16:17, four]

    @pl.when(i == NCH - 1)
    def _():
        e_ref[...] = state[0:17, :]


def whole(shape):
    return pl.BlockSpec(shape, lambda *_: (0,) * len(shape))


def smem():
    return pl.BlockSpec(memory_space=pltpu.SMEM)


def tokens(width):
    return pl.BlockSpec((Q, width), lambda i: (i, 0))


def across(rows):
    return pl.BlockSpec((rows, Q), lambda i: (0, i))


def local(doc_lengths, me, x, step_t, rate, b_t, c_t, skip):
    return pl.pallas_call(
        local_kernel,
        grid=(NCH,),
        in_specs=[
            smem(), smem(), tokens(4096), across(64), whole((1, 64)), across(16), across(16), smem(),
        ],
        out_specs=[tokens(4096), whole((17, 4096))],
        scratch_shapes=[pltpu.VMEM((24, 4096), jnp.float32)],
        out_shape=[
            jax.ShapeDtypeStruct((512, 4096), jnp.bfloat16),
            jax.ShapeDtypeStruct((17, 4096), jnp.float32),
        ],
        compiler_params=PARAMS,
        cost_estimate=SMALL,
        name="scan_local",
    )(doc_lengths, me, x, step_t, rate, b_t, c_t, skip)


def gate_kernel(
    len_ref, me_ref, y_ref, g_ref, step_ref, rate_ref, c_ref, h_ref, o_ref, row_ref, prefix,
):
    i = pl.program_id(0)
    base = me_ref[0] * 512

    @pl.when(i == 0)
    def _():
        prefix[...] = jnp.zeros_like(prefix)

    r, c = eye_like()
    eye = jnp.where(c == r, 1.0, 0.0).astype(jnp.bfloat16)
    _, end_before = last_doc(len_ref, base - 1)
    ct = cumulate(step_ref[...], rate_ref[...] * LOG2E) + prefix[0:1, :]
    prefix[0:1, :] = ct[Q - 1 : Q, :]
    c_rows = dot_t(eye, c_ref[...]).astype(jnp.bfloat16)
    cc2 = jnp.concatenate([c_rows, c_rows], axis=1)
    low = lax.broadcasted_iota(jnp.int32, (Q, 128), 1) < 64
    enter = base + i * Q + lax.broadcasted_iota(jnp.int32, (Q, 128), 0) < end_before
    sq = jnp.zeros((Q, 128), jnp.float32)
    for w in range(16):
        from_state = dot(cc2, split_rows(h_ref[:, w * 256 : (w + 1) * 256]))
        for pair in range(2):
            h0 = w * 4 + pair * 2
            col = slice(h0 * 64, h0 * 64 + 128)
            e = jnp.exp2(
                jnp.where(
                    low,
                    jnp.broadcast_to(ct[:, h0 : h0 + 1], (Q, 128)),
                    jnp.broadcast_to(ct[:, h0 + 1 : h0 + 2], (Q, 128)),
                )
            )
            y = y_ref[:, col].astype(jnp.float32) + jnp.where(enter, e, 0.0) * (
                from_state[:, pair * 128 : (pair + 1) * 128]
            )
            g = 0.5 * g_ref[:, col].astype(jnp.float32)
            v = y * (g + g * jnp.tanh(g))
            sq = sq + v * v
            o_ref[:, col] = v.astype(o_ref.dtype)
    row_ref[...] = jnp.sum(sq.T, axis=0, keepdims=True)


def gate(doc_lengths, me, y, g, step_t, rate, c_t, h):
    return pl.pallas_call(
        gate_kernel,
        grid=(NCH,),
        in_specs=[
            smem(), smem(), tokens(4096), tokens(4096), across(64), whole((1, 64)), across(16),
            whole((16, 4096)),
        ],
        out_specs=[tokens(4096), across(1)],
        scratch_shapes=[pltpu.VMEM((8, 64), jnp.float32)],
        out_shape=[
            jax.ShapeDtypeStruct((512, 4096), jnp.bfloat16),
            jax.ShapeDtypeStruct((1, 512), jnp.float32),
        ],
        compiler_params=PARAMS,
        cost_estimate=SMALL,
        name="scan_gate",
    )(doc_lengths, me, y, g, step_t, rate, c_t, h)


NB = 128


def norm_kernel(v_ref, s0, s1, s2, s3, gain_ref, o_ref):
    row = lax.rsqrt((s0[...] + s1[...] + s2[...] + s3[...]) / INNER + 1e-05)
    factor = row_to_column(row)
    for w in range(4096 // 128):
        col = slice(w * 128, (w + 1) * 128)
        o_ref[:, col] = (v_ref[:, col].astype(jnp.float32) * factor * gain_ref[:, col]).astype(
            o_ref.dtype
        )


def norm(v, sums, gain):
    rows = pl.BlockSpec((NB, 4096), lambda i: (i, 0))
    return pl.pallas_call(
        norm_kernel,
        grid=(512 // NB,),
        in_specs=[rows] + [pl.BlockSpec((1, NB), lambda i: (0, i))] * 4 + [whole((1, 4096))],
        out_specs=rows,
        out_shape=jax.ShapeDtypeStruct((512, 4096), jnp.bfloat16),
        compiler_params=pltpu.CompilerParams(vmem_limit_bytes=16 * 2**20),
        cost_estimate=SMALL,
        name="norm",
    )(v, *sums, gain)


def pack_kernel(k_ref, v_ref, o_ref):
    o_ref[:, 0:256] = k_ref[...]
    o_ref[:, 256:512] = v_ref[...]


def pack(keys, values):
    return pl.pallas_call(
        pack_kernel,
        out_shape=jax.ShapeDtypeStruct((512, 512), jnp.bfloat16),
        compiler_params=pltpu.CompilerParams(vmem_limit_bytes=8 * 2**20),
        cost_estimate=SMALL,
        name="pack",
    )(keys, values)


def attention_kernel(
    len_ref, plan_ref, me_ref, q_hbm, *rest
):
    kv = rest[:9]
    o_hbm, q_ref, o_ref, kv_buf, ka, ve, ohq, s_a, s_b, causal, order, sem = rest[9:]
    bring = pltpu.make_async_copy(q_hbm, q_ref, sem.at[4])
    bring.start()
    me = me_ref[0]
    core = lax.rem(me, 2)
    open_doc, _ = last_doc(len_ref, me * 512)
    order[0] = 0
    n_act = jnp.int32(1)
    for m in range(1, 4):
        off = plan_ref[m, me]
        order[n_act] = off
        n_act = n_act + jnp.where((off <= me) & (open_doc <= (me - off) * 512 + 511), 1, 0)
    for j in range(4):

        @pl.when(j < n_act)
        def _(j=j):
            off = order[j]
            source = jnp.where(lax.rem(off, 2) == 0, off // 2, 4 + (off + 1 - core) // 2)
            for k in range(9):

                @pl.when(source == k)
                def _(k=k):
                    pltpu.make_async_copy(kv[k], kv_buf.at[j], sem.at[j]).start()

    starts, ends = doc_rows(len_ref)
    ohq[...] = jnp.where(one_hot(me * 512, 512, starts, ends), 1.0, 0.0).astype(jnp.bfloat16)
    r = lax.broadcasted_iota(jnp.int32, (TQ, TQ), 0)
    c = lax.broadcasted_iota(jnp.int32, (TQ, TQ), 1)
    causal[...] = jnp.where(c <= r, 0.0, -1e30)
    for j in range(4):

        @pl.when(j < n_act)
        def _(j=j):
            pltpu.make_async_copy(kv[0], kv_buf.at[j], sem.at[j]).wait()
            same = one_hot((me - order[j]) * 512, 512, starts, ends)
            bias = jnp.where(same, 0.0, -BIG).astype(jnp.bfloat16)
            for g in range(2):
                ka[g, j, :, 0:128] = kv_buf[j, :, g * 128 : (g + 1) * 128]
                ka[g, j, :, 128:256] = bias
                ve[g, j, :, 0:128] = kv_buf[j, :, 256 + g * 128 : 256 + (g + 1) * 128]
                ve[g, j, :, 128:256] = jnp.ones((512, 128), jnp.bfloat16)

    bring.wait()
    factor = jnp.float32(128**-0.5 * LOG2E)

    def variant(n):
        def score(h, t, s_ref):
            g = h // 8
            col = pl.multiple_of(h * 128, 128)
            own = slice(t * TQ, (t + 1) * TQ)
            qa = jnp.concatenate([q_ref[own, pl.ds(col, 128)], ohq[own, :]], axis=1)
            at = 0
            if t > 0:
                s_ref[:, 0:TQ] = dot_t(qa, ka[g, 0, 0:TQ, :])
                at = TQ
            s_ref[:, at : at + TQ] = dot_t(qa, ka[g, 0, own, :]) + causal[...]
            at += TQ
            for j in range(1, n):
                s_ref[:, at : at + 512] = dot_t(qa, ka[g, j])
                at += 512

        def soft(h, t, s_ref):
            g = h // 8
            width = (t + 1) * TQ + 512 * (n - 1)
            peak = s_ref[:, 0:128]
            for k in range(1, width // 128):
                peak = jnp.maximum(peak, s_ref[:, k * 128 : (k + 1) * 128])
            peak = jnp.max(peak, axis=1, keepdims=True) * factor
            at = 0
            total = None
            for j, rows in [(0, (t + 1) * TQ)] + [(j, 512) for j in range(1, n)]:
                w = jnp.exp2(s_ref[:, at : at + rows] * factor - peak).astype(jnp.bfloat16)
                at += rows
                part = dot(w, ve[g, j, 0:rows, :])
                total = part if total is None else total + part
            col = pl.multiple_of(h * 128, 128)
            o_ref[t * TQ : (t + 1) * TQ, pl.ds(col, 128)] = (
                total[:, :128] / total[:, 128:]
            ).astype(jnp.bfloat16)

        score(0, 0, s_a)

        def body(h, _):
            score(h, 1, s_b)
            soft(h, 0, s_a)
            score(jnp.minimum(h + 1, 15), 0, s_a)
            soft(h, 1, s_b)
            return 0

        lax.fori_loop(0, 8, body, 0)
        halves[0].start()
        lax.fori_loop(8, 16, body, 0)
        halves[1].start()

    halves = [
        pltpu.make_async_copy(o_ref.at[:, part], o_hbm.at[:, part], sem.at[5 + p])
        for p, part in enumerate((slice(0, 1024), slice(1024, 2048)))
    ]
    for n in range(1, 5):

        @pl.when(n_act == n)
        def _(n=n):
            variant(n)

    halves[0].wait()
    halves[1].wait()


def attention(doc_lengths, plan, me, q, blocks):
    return pl.pallas_call(
        attention_kernel,
        in_specs=[smem(), smem(), smem()] + [pl.BlockSpec(memory_space=pl.ANY)] * 10,
        out_specs=pl.BlockSpec(memory_space=pl.ANY),
        scratch_shapes=[
            pltpu.VMEM((512, 2048), jnp.bfloat16),
            pltpu.VMEM((512, 2048), jnp.bfloat16),
            pltpu.VMEM((4, 512, 512), jnp.bfloat16),
            pltpu.VMEM((2, 4, 512, 256), jnp.bfloat16),
            pltpu.VMEM((2, 4, 512, 256), jnp.bfloat16),
            pltpu.VMEM((512, 128), jnp.bfloat16),
            pltpu.VMEM((TQ, 2048), jnp.float32),
            pltpu.VMEM((TQ, 2048), jnp.float32),
            pltpu.VMEM((TQ, TQ), jnp.float32),
            pltpu.SMEM((4,), jnp.int32),
            pltpu.SemaphoreType.DMA((7,)),
        ],
        out_shape=jax.ShapeDtypeStruct((512, 2048), jnp.bfloat16),
        compiler_params=PARAMS,
        cost_estimate=pl.CostEstimate(flops=3 * 10**10, bytes_accessed=10**7, transcendentals=0),
        name="attention",
    )(doc_lengths, plan, me, q, *blocks)


def chip_pairs(move):
    return [
        (i, j)
        for i in range(32)
        for j in [move(i // 8, (i // 2) % 4, i % 2)]
        if j is not None
    ]


def spot(z, y, c):
    return (z * 4 + y % 4) * 2 + c if 0 <= z < 4 else None


def along_y(x, by):
    return lax.ppermute(x, "ctx", chip_pairs(lambda z, y, c: spot(z, y + by, c)))


def along_z(x):
    return lax.ppermute(x, "ctx", chip_pairs(lambda z, y, c: spot(z + 1, y, c)))


def swap_cores(x):
    return lax.ppermute(x, "ctx", [(i, i ^ 1) for i in range(32)])


def chips_back(x, by):
    return lax.ppermute(x, "ctx", [(i, i + 2 * by) for i in range(32 - 2 * by)])


def carry_state(state, core, beside):
    half = state.shape[1] // 2
    left, right = state[:17, :half], state[:17, half:]
    mine = jnp.where(core == 0, left, right)
    got = swap_cores(jnp.where(core == 0, right, left))
    first = jnp.where(core == 0, mine, got)
    later = jnp.where(core == 0, got, mine)
    e0, t0 = first[:16], first[16:]
    e1, t1 = later[:16], later[16:]
    chip = jnp.concatenate([e1 + t1 * e0, t0 * t1], axis=0)
    parts = [chips_back(chip, by) for by in (1, 2, 3, 4)]
    held = parts[3][:16]
    for part in parts[2::-1]:
        held = part[:16] + part[16:] * held
    second = e0 + t0 * held
    held, second, beside = lax.optimization_barrier((held, second, beside))
    keep = jnp.where(core == 0, held, second)
    got = swap_cores(jnp.where(core == 0, second, held))
    return jnp.concatenate(
        [jnp.where(core == 0, keep, got), jnp.where(core == 0, got, keep)], axis=1
    ), beside


def shards(
    queries,
    keys,
    values,
    block_plan,
    doc_lengths,
    scan_input,
    gate_input,
    step_size,
    decay_rate,
    state_in,
    state_out,
    skip_gain,
    norm_gain,
):
    me = lax.axis_index("ctx")
    core = me % 2
    row = (me // 2) % 4
    kv = pack(keys, values)
    above = along_z(kv)
    swapped = swap_cores(kv)
    me1 = me.reshape(1)
    step_t = step_size.T
    rate = decay_rate[None]
    c_t = state_out.T
    y, state = local(
        doc_lengths, me1, scan_input, step_t, rate, state_in.T, c_t, skip_gain
    )
    state, above = lax.optimization_barrier((state, above))
    same = {by: along_y(jnp.where(row + by < 4, kv, above), by) for by in (1, 3, 2)}
    incoming, near = carry_state(state, core, same[1])
    gated, squares = gate(
        doc_lengths, me1, y, gate_input, step_t, rate, c_t, incoming
    )
    sums = [squares] + [
        lax.ppermute(squares, "tp", [(i, (i + by) % 4) for i in range(4)]) for by in (1, 3, 2)
    ]
    sums, near, low, far_one, above = lax.optimization_barrier(
        (sums, near, same[3], same[2], above)
    )
    blocks = [kv, near, far_one, low, swapped]
    blocks += [swap_cores(b) for b in (near, far_one, low, above)]
    attn_out = attention(doc_lengths, block_plan.T, me1, queries, blocks)
    gated, attn_out = lax.optimization_barrier((gated, attn_out))
    mamba_out = norm(gated, sums, norm_gain[None])
    return (attn_out, mamba_out)


def solution(mesh):
    in_specs = (
        P("ctx", "tp"),
        P("ctx", "tp"),
        P("ctx", "tp"),
        P(),
        P(),
        P("ctx", "tp"),
        P("ctx", "tp"),
        P("ctx", "tp"),
        P("tp"),
        P("ctx", None),
        P("ctx", None),
        P("tp"),
        P("tp"),
    )
    out_specs = (P("ctx", "tp"), P("ctx", "tp"))
    return jax.shard_map(shards, mesh=mesh, in_specs=in_specs, out_specs=out_specs, check_vma=False)
```
